256 devices in a mesh: dp: 64 (over y, x_lo, z), group: 4 (over x_hi, core).
Axes of the slice: x: 4 (x_hi: 2, x_lo: 2; x = x_hi * 2 + x_lo), y: 4, z: 8, core: 2. Of those that a mesh axis runs over, the one named last changes fastest.
Arguments:
- activations: bfloat16 [2, 24576, 5120], P(None, 'dp')
- tile_owner: int32 [55], replicated, may hold values from 0 to 63, as said below
- gradient: bfloat16 [10, 512, 4096], P(None, 'dp', 'group'), may hold values from -6 to 6
- block_owner: int32 [10], replicated, may hold values from 0 to 63, as said below
- eigen_basis: bfloat16 [128, 512, 512], P('dp'), may hold values from -0.25 to 0.25
- eigen_values: float32 [128, 512], P('dp'), may hold values from 0.05 to 5
Outputs:
- factor_tiles: float32 [128, 512, 512], P('dp', None, 'group')
- preconditioned: bfloat16 [10, 512, 4096], P(None, 'dp', 'group')
The draws below stay inside these ranges and needn't reach their ends.
Inputs may be any that keep to these rules, and one draw needn't show every extreme that they name: `tile_owner`: no owner holds more than 2 tiles, and some owner holds exactly 2. `block_owner`: no owner holds more than 2 blocks, and some owner holds exactly 2.
All inputs are finite; a program needn't handle non-finite values.
Results may differ from the reference program's by a relative error of at most 0.0043.
Values may be sent and summed in bfloat16 or wider, within the bound.
No kernel may reach another device: no remote copies, remote signals or barrier semaphores. Data moves between devices by JAX's collectives and lax.ppermute only.
A program may use at most 128 MiB of HBM per device.

```python
import math
import jax
import jax.numpy as jnp
import numpy as np
from jax import lax

D = 5120
TILE = 512
QO = 4096
MB = 2
NT = 10
UT = 55
SL = 2
GS = 2
TOKENS = 24576
N_DP = 64


def owner_list(key, entries, capacity):
    slots_total = N_DP * capacity
    key_order, key_shuffle = jax.random.split(key)
    order = jax.random.permutation(key_order, slots_total)
    owners_all = order // capacity
    favoured = owners_all[0]
    score = jnp.where(owners_all == favoured, 0, 1) * slots_total + jnp.arange(slots_total)
    picked = order[jnp.argsort(score, stable=True)][:entries]
    shuffle = jax.random.permutation(key_shuffle, entries)
    return (picked[shuffle] // capacity).astype(jnp.int32)


def draw_tile_owner(key, part):
    key = jax.random.fold_in(key, 3)
    return owner_list(key, UT, SL)


def draw_block_owner(key, part):
    key = jax.random.fold_in(key, 5)
    return owner_list(key, NT, GS)


def draw_activations(key, part):
    key = jax.random.fold_in(key, 11)
    key_noise, key_col, key_row = jax.random.split(key, 3)
    shape = (MB, TOKENS, D)
    column_scale = jnp.exp(jax.random.uniform(key_col, (D,), jnp.float32, math.log(0.3), math.log(3.0)))
    row_scale = jnp.exp(jax.random.uniform(key_row, (MB, TOKENS, 1), jnp.float32, math.log(0.5), math.log(2.0)))
    noise = jax.random.normal(key_noise, shape, jnp.float32)
    values = noise * column_scale * row_scale
    return values.astype(jnp.bfloat16)


def block_levels(stream_key, shape, shards, least, largest):
    loudness, own = 1.0, jax.random.fold_in(stream_key, 6)
    for axis_at, parts in shards:
        draws = jnp.exp(jax.random.uniform(jax.random.fold_in(own, axis_at), (parts,), jnp.float32, least / len(shards), largest / len(shards)))
        loudness = loudness * jnp.repeat(draws, shape[axis_at] // parts).reshape([-1 if axis == axis_at else 1 for axis in range(len(shape))])
    return loudness


def gaussian(stream_key, dims, deviation, most, pieces=(), kind=jnp.bfloat16):
    loudness = block_levels(stream_key, dims, pieces, -0.22, 0.18) if pieces else 1.0
    values = jax.random.normal(stream_key, dims, jnp.float32) * deviation * loudness
    return jnp.minimum(jnp.maximum(values, -most), most).astype(kind)


def setup_inputs(seed: int = 0) -> dict:
    keys = jax.random.split(jax.random.key(seed), 7)
    activations = draw_activations(jax.random.fold_in(keys[6], 71), 0)
    tile_owner = draw_tile_owner(jax.random.fold_in(keys[6], 71), 0)
    gradient = gaussian(keys[2], (NT, TILE, QO), 1.0, 6.0, ((1, 64), (2, 4)))
    block_owner = draw_block_owner(jax.random.fold_in(keys[6], 71), 0)
    eigen_basis = gaussian(keys[4], (N_DP * GS, TILE, TILE), TILE ** -0.5, 0.25, ((0, 64),))
    eigen_values = jnp.clip(jnp.exp(math.log(5.0) - 4.6051702 * jax.random.uniform(keys[5], (N_DP * GS, TILE), jnp.float32) ** block_levels(keys[5], (N_DP * GS, TILE), ((0, 64),), -0.2, 0.2)), 0.05, 5.0)
    return dict(activations=activations, tile_owner=tile_owner, gradient=gradient, block_owner=block_owner, eigen_basis=eigen_basis, eigen_values=eigen_values)


damping = 0.1


def slot_rank(owner_ids):
    entries = owner_ids.shape[0]
    position = jnp.arange(entries)
    same_owner = owner_ids[:, None] == owner_ids[None, :]
    earlier = position[None, :] < position[:, None]
    return jnp.sum(jnp.logical_and(same_owner, earlier), axis=1).astype(jnp.int32)


def reference(activations, tile_owner, gradient, block_owner, eigen_basis, eigen_values):
    summed = jnp.zeros((D, D), jnp.float32)
    for micro in range(MB):
        values = activations[micro].astype(jnp.float32)
        summed = summed + jnp.dot(values.T, values, precision=lax.Precision.HIGHEST)
    covariance = summed / (MB * TOKENS)
    first_index, second_index = np.triu_indices(NT)
    tile_values = covariance.reshape(NT, TILE, NT, TILE).transpose(0, 2, 1, 3)[first_index, second_index]
    target = (tile_owner * SL + slot_rank(tile_owner)).astype(jnp.int32)
    factor = jnp.zeros((N_DP * SL, TILE, TILE), jnp.float32).at[target].set(tile_values)
    block_slot = (block_owner * GS + slot_rank(block_owner)).astype(jnp.int32)
    chosen_basis = eigen_basis[block_slot].astype(jnp.float32)
    turned = jnp.einsum("bkr,bkc->brc", chosen_basis, gradient.astype(jnp.float32), precision=lax.Precision.HIGHEST)
    scaled = (turned / (eigen_values[block_slot][:, :, None] + damping)).astype(jnp.bfloat16).astype(jnp.float32)
    result = jnp.einsum("bkr,brc->bkc", chosen_basis, scaled, precision=lax.Precision.HIGHEST)
    return factor, result.astype(jnp.bfloat16)
```

```python
import functools

import jax
import jax.numpy as jnp
import numpy as np
from jax import lax
from jax.experimental import pallas as pl
from jax.experimental.pallas import tpu as pltpu
from jax.sharding import Mesh, PartitionSpec as P

TILE = 512
NT = 10
UT = NT * (NT + 1) // 2
SLOTS = 2
SLAB = 128
FIRST_ROWS = 3
FIRST_TILES = sum(NT - i for i in range(FIRST_ROWS))
LAST_TILES = UT - FIRST_TILES
DP = ("y", "xl", "z")

damping = 0.1
bf16 = jnp.bfloat16
f32 = jnp.float32


def slot_rank(owner_ids):
    entries = owner_ids.shape[0]
    position = jnp.arange(entries)
    same_owner = owner_ids[:, None] == owner_ids[None, :]
    earlier = position[None, :] < position[:, None]
    return jnp.sum(jnp.logical_and(same_owner, earlier), axis=1)


def dot(a, b):
    return lax.dot_general(a, b, (((1,), (0,)), ((), ())), preferred_element_type=f32)


def first_kernel(place, act, own, near, far, slab, other, turned):
    low, mine, theirs = place[0], place[1], place[2]
    for j in range(NT):
        at = j * TILE
        slab[:, j * SLAB : (j + 1) * SLAB] = act[:, pl.ds(pl.multiple_of(at + mine * SLAB, SLAB), SLAB)]
        other[:, j * SLAB : (j + 1) * SLAB] = act[:, pl.ds(pl.multiple_of(at + theirs * SLAB, SLAB), SLAB)]
    start = 0
    for i in range(FIRST_ROWS):
        for q in range(4):
            row = pl.multiple_of(lax.rem(q + 2 * low, 4) * SLAB, SLAB)
            turned[pl.ds(row, SLAB), :] = act[:, i * TILE + q * SLAB : i * TILE + (q + 1) * SLAB].T
        for begin in range(i * SLAB, NT * SLAB, 256):
            end = min(begin + 256, NT * SLAB)
            to = slice(start, start + end - begin)
            kept = dot(turned[0:384, :], slab[:, begin:end])
            own[:, to] = kept[0:256]
            near[:, to] = kept[256:384].astype(bf16)
            far[:, to] = dot(turned[384:512, :], other[:, begin:end]).astype(bf16)
            start += end - begin


def last_kernel(place, act, out, slab, turned):
    mine = place[1]
    for j in range(FIRST_ROWS, NT):
        slab[:, j * SLAB : (j + 1) * SLAB] = act[:, pl.ds(pl.multiple_of(j * TILE + mine * SLAB, SLAB), SLAB)]
    start = 0
    for i in range(FIRST_ROWS, NT):
        turned[...] = act[:, i * TILE : (i + 1) * TILE].T
        for begin in range(i * SLAB, NT * SLAB, 256):
            end = min(begin + 256, NT * SLAB)
            out[:, start : start + end - begin] = dot(turned[...], slab[:, begin:end])
            start += end - begin


def first_products(act, place):
    tokens = act.shape[0]
    wide = FIRST_TILES * SLAB
    vmem = pl.BlockSpec(memory_space=pltpu.VMEM)
    return pl.pallas_call(
        first_kernel,
        out_shape=(
            jax.ShapeDtypeStruct((256, wide), f32),
            jax.ShapeDtypeStruct((128, wide), bf16),
            jax.ShapeDtypeStruct((128, wide), bf16),
        ),
        in_specs=[pl.BlockSpec(memory_space=pltpu.SMEM), vmem],
        out_specs=(vmem, vmem, vmem),
        scratch_shapes=[
            pltpu.VMEM((tokens, NT * SLAB), bf16),
            pltpu.VMEM((tokens, NT * SLAB), bf16),
            pltpu.VMEM((TILE, tokens), bf16),
        ],
        compiler_params=pltpu.CompilerParams(vmem_limit_bytes=40 * 2**20),
        cost_estimate=pl.CostEstimate(
            flops=2 * tokens * TILE * wide, bytes_accessed=act.size * 2 + 768 * wide * 2, transcendentals=0
        ),
    )(place, act)


def last_products(act, place):
    tokens = act.shape[0]
    wide = LAST_TILES * SLAB
    vmem = pl.BlockSpec(memory_space=pltpu.VMEM)
    return pl.pallas_call(
        last_kernel,
        out_shape=jax.ShapeDtypeStruct((TILE, wide), f32),
        in_specs=[pl.BlockSpec(memory_space=pltpu.SMEM), vmem],
        out_specs=vmem,
        scratch_shapes=[
            pltpu.VMEM((tokens, NT * SLAB), bf16),
            pltpu.VMEM((TILE, tokens), bf16),
        ],
        compiler_params=pltpu.CompilerParams(vmem_limit_bytes=40 * 2**20),
        cost_estimate=pl.CostEstimate(
            flops=2 * tokens * TILE * wide, bytes_accessed=act.size * 2 + TILE * wide * 4, transcendentals=0
        ),
    )(place, act)


def around_z(product):
    n = lax.axis_size("z")
    z = lax.axis_index("z")
    rows = product.shape[0] // n
    half = rows // 2
    up = [(i, (i + 1) % n) for i in range(n)]
    down = [(i, (i - 1) % n) for i in range(n)]

    def chunk(k):
        return lax.dynamic_slice_in_dim(product, lax.rem(z + (k + n), n) * rows, rows, 0)

    ahead = lax.ppermute(chunk(n // 2)[:half].astype(bf16), "z", up)
    back = lax.ppermute(chunk(n // 2)[half:].astype(bf16), "z", down)
    ahead = jnp.concatenate([ahead, jnp.zeros_like(ahead)], axis=0)
    back = jnp.concatenate([jnp.zeros_like(back), back], axis=0)
    for k in range(n // 2 - 1, 0, -1):
        ahead = lax.ppermute((chunk(k) + ahead.astype(f32)).astype(bf16), "z", up)
        back = lax.ppermute((chunk(-k) + back.astype(f32)).astype(bf16), "z", down)
    return chunk(0) + ahead.astype(f32) + back.astype(f32)


def scatter_sum(x, axis):
    n = lax.axis_size(axis)
    got = lax.all_to_all(x.astype(bf16), axis, split_axis=0, concat_axis=0, tiled=True)
    return jnp.sum(got.reshape(n, x.shape[0] // n, x.shape[1]).astype(f32), axis=0)


def factor_shares(activations):
    micro, tokens, width = activations.shape
    act = activations.reshape(micro * tokens, width)
    low = lax.axis_index("xl")
    high, core = lax.axis_index("xh"), lax.axis_index("c")
    place = jnp.stack([low, high * 2 + core, (1 - high) * 2 + core]).astype(jnp.int32)
    own, near, far = first_products(act, place)
    near = lax.ppermute(near, "xl", [(0, 1), (1, 0)])
    far = lax.ppermute(far, ("xl", "xh"), [(i, 3 - i) for i in range(4)])
    last = last_products(act, place)

    last = around_z(last)
    half = last.shape[0] // 2
    sent = lax.dynamic_slice_in_dim(last, (1 - low) * half, half, 0)
    kept = lax.dynamic_slice_in_dim(last, low * half, half, 0)
    last = kept + lax.ppermute(sent.astype(bf16), "xl", [(0, 1), (1, 0)]).astype(f32)
    last = scatter_sum(last, "y")

    first = own + jnp.concatenate([near, far], axis=0).astype(f32)
    first = scatter_sum(first, "y")
    first = scatter_sum(first, "z")
    return jnp.concatenate([first, last], axis=1)


def factor_part(activations, tile_owner):
    dp_count = lax.axis_size(DP)
    total = activations.shape[0] * activations.shape[1] * dp_count
    rows = TILE // dp_count
    rank = slot_rank(tile_owner)
    shares = factor_shares(activations) / total
    destination = rank * dp_count + tile_owner
    selector = (destination[None, :] == jnp.arange(SLOTS * dp_count)[:, None]).astype(bf16)
    packed = jnp.einsum(
        "pu,rus->prs", selector, shares.astype(bf16).reshape(rows, UT, SLAB), preferred_element_type=f32
    ).astype(bf16)
    packed = packed.reshape(SLOTS, dp_count, rows, SLAB)
    arrived = lax.all_to_all(packed, DP, split_axis=1, concat_axis=1, tiled=True)
    ny, nx, nz = (lax.axis_size(a) for a in DP)
    arrived = arrived.reshape(SLOTS, ny, nx, nz, rows, SLAB)
    me = lax.axis_index(DP)
    slot = jnp.arange(SLOTS)
    held = (tile_owner[None, :] == me) & (rank[None, :] == slot[:, None])
    is_first = jnp.any(held & (jnp.arange(UT) < FIRST_TILES)[None, :], axis=1)
    as_first = arrived.transpose(0, 2, 1, 3, 4, 5).reshape(SLOTS, TILE, SLAB)
    as_last = arrived.transpose(0, 3, 2, 1, 4, 5).reshape(SLOTS, TILE, SLAB)
    return jnp.where(is_first[:, None, None], as_first, as_last).astype(f32)


def precondition_blocks(gradient, block_owner, eigen_basis, eigen_values):
    dp_count = lax.axis_size(DP)
    slot_count = eigen_basis.shape[0]
    block_count, row_count, col_total = gradient.shape
    destination = slot_rank(block_owner) * dp_count + block_owner
    selector = (destination[None, :] == jnp.arange(slot_count * dp_count)[:, None]).astype(bf16)
    packed = jnp.einsum("pn,nrq->prq", selector, gradient, preferred_element_type=f32)
    packed = packed.astype(bf16).reshape(slot_count, dp_count, row_count, col_total)
    received = lax.all_to_all(packed, DP, split_axis=1, concat_axis=1, tiled=True)
    col_count = received.shape[3]
    blocks = received.reshape(slot_count, dp_count * row_count, col_count)
    turned = jnp.einsum("gkr,gkc->grc", eigen_basis, blocks, preferred_element_type=f32)
    scaled = (turned / (eigen_values[:, :, None] + damping)).astype(bf16)
    rotated = jnp.einsum("gkr,grc->gkc", eigen_basis, scaled, preferred_element_type=f32)
    rotated = rotated.astype(bf16).reshape(slot_count, dp_count, row_count, col_count)
    returned = lax.all_to_all(rotated, DP, split_axis=1, concat_axis=1, tiled=True)
    flattened = returned.reshape(slot_count * dp_count, row_count, col_total)
    result = jnp.einsum("pn,prq->nrq", selector, flattened, preferred_element_type=f32)
    return result.astype(bf16)


def shards(activations, tile_owner, gradient, block_owner, eigen_basis, eigen_values):
    factor = factor_part(activations, tile_owner)
    result = precondition_blocks(gradient, block_owner, eigen_basis, eigen_values)
    return (factor, result)


def solution(mesh):
    fine = Mesh(mesh.devices.reshape(4, 2, 8, 2, 2), ("y", "xl", "z", "xh", "c"))
    group = ("xh", "c")
    placed = (
        P(None, DP, None),
        P(),
        P(None, DP, group),
        P(),
        P(DP, None, None),
        P(DP, None),
    )
    return jax.shard_map(
        shards,
        mesh=fine,
        in_specs=placed,
        out_specs=(P(DP, None, group), P(None, DP, group)),
        check_vma=False,
    )
```

```python
import functools

import jax
import jax.numpy as jnp
import numpy as np
from jax import lax
from jax.experimental import pallas as pl
from jax.experimental.pallas import tpu as pltpu
from jax.sharding import Mesh, PartitionSpec as P

TILE = 512
NT = 10
UT = NT * (NT + 1) // 2
SLOTS = 2
SLAB = 128
FIRST_ROWS = 3
FIRST_TILES = sum(NT - i for i in range(FIRST_ROWS))
LAST_TILES = UT - FIRST_TILES
DP = ("y", "xl", "z")

damping = 0.1
bf16 = jnp.bfloat16
f32 = jnp.float32


def slot_rank(owner_ids):
    entries = owner_ids.shape[0]
    position = jnp.arange(entries)
    same_owner = owner_ids[:, None] == owner_ids[None, :]
    earlier = position[None, :] < position[:, None]
    return jnp.sum(jnp.logical_and(same_owner, earlier), axis=1)


def dot(a, b):
    return lax.dot_general(a, b, (((1,), (0,)), ((), ())), preferred_element_type=f32)


def fill(slab, act, which, begin):
    for j in range(begin, NT):
        at = pl.multiple_of(j * TILE + which * SLAB, SLAB)
        slab[:, j * SLAB : (j + 1) * SLAB] = act[:, pl.ds(at, SLAB)]


def spans(i):
    return [(at, min(at + 256, NT * SLAB)) for at in range(i * SLAB, NT * SLAB, 256)]


def sent_kernel(place, act, near, far, out, slab, other, turned):
    low, mine, theirs = place[0], place[1], place[2]
    fill(slab, act, mine, 0)
    fill(other, act, theirs, 0)
    start = 0
    for i in range(FIRST_ROWS):
        at = pl.multiple_of(i * TILE + (1 - low) * 256, 256)
        turned[0:256, :] = act[:, pl.ds(at, 256)].T
        for begin, end in spans(i):
            to = slice(start, start + end - begin)
            near[:, to] = dot(turned[0:128, :], slab[:, begin:end]).astype(bf16)
            far[:, to] = dot(turned[128:256, :], other[:, begin:end]).astype(bf16)
            start += end - begin
    start = 0
    for i in range(FIRST_ROWS, NT):
        turned[...] = act[:, i * TILE : (i + 1) * TILE].T
        for begin, end in spans(i):
            out[:, start : start + end - begin] = dot(turned[...], slab[:, begin:end])
            start += end - begin


def kept_kernel(place, act, own, slab, turned):
    low, mine = place[0], place[1]
    fill(slab, act, mine, 0)
    start = 0
    for i in range(FIRST_ROWS):
        turned[...] = act[:, pl.ds(pl.multiple_of(i * TILE + low * 256, 256), 256)].T
        for begin, end in spans(i):
            own[:, start : start + end - begin] = dot(turned[...], slab[:, begin:end])
            start += end - begin


VMEM = pl.BlockSpec(memory_space=pltpu.VMEM)
SMEM = pl.BlockSpec(memory_space=pltpu.SMEM)


def call(kernel, outs, scratch, flops, *operands, scalars=1):
    moved = sum(x.size * x.dtype.itemsize for x in operands)
    moved += sum(x.size * x.dtype.itemsize for x in outs)
    return pl.pallas_call(
        kernel,
        out_shape=tuple(outs),
        in_specs=[SMEM] * scalars + [VMEM] * (len(operands) - scalars),
        out_specs=(VMEM,) * len(outs),
        scratch_shapes=[pltpu.VMEM(shape, dtype) for shape, dtype in scratch],
        compiler_params=pltpu.CompilerParams(vmem_limit_bytes=40 * 2**20),
        cost_estimate=pl.CostEstimate(flops=flops, bytes_accessed=moved, transcendentals=0),
    )(*operands)


def array(shape, dtype):
    return jax.ShapeDtypeStruct(shape, dtype)


def sent_products(act, place):
    tokens = act.shape[0]
    wide, rest = FIRST_TILES * SLAB, LAST_TILES * SLAB
    return call(
        sent_kernel,
        [array((128, wide), bf16), array((128, wide), bf16), array((TILE, rest), f32)],
        [((tokens, NT * SLAB), bf16), ((tokens, NT * SLAB), bf16), ((TILE, tokens), bf16)],
        2 * tokens * (256 * wide + TILE * rest),
        place,
        act,
    )


def kept_products(act, place):
    tokens = act.shape[0]
    wide = FIRST_TILES * SLAB
    [own] = call(
        kept_kernel,
        [array((256, wide), f32)],
        [((tokens, NT * SLAB), bf16), ((256, tokens), bf16)],
        2 * tokens * 256 * wide,
        place,
        act,
    )
    return own


def around_z(product):
    n = lax.axis_size("z")
    z = lax.axis_index("z")
    rows = product.shape[0] // n
    half = rows // 2
    up = [(i, (i + 1) % n) for i in range(n)]
    down = [(i, (i - 1) % n) for i in range(n)]

    def chunk(k):
        return lax.dynamic_slice_in_dim(product, lax.rem(z + (k + n), n) * rows, rows, 0)

    ahead = lax.ppermute(chunk(n // 2)[:half].astype(bf16), "z", up)
    back = lax.ppermute(chunk(n // 2)[half:].astype(bf16), "z", down)
    ahead = jnp.concatenate([ahead, jnp.zeros_like(ahead)], axis=0)
    back = jnp.concatenate([jnp.zeros_like(back), back], axis=0)
    for k in range(n // 2 - 1, 0, -1):
        ahead = lax.ppermute((chunk(k) + ahead.astype(f32)).astype(bf16), "z", up)
        back = lax.ppermute((chunk(-k) + back.astype(f32)).astype(bf16), "z", down)
    return chunk(0) + ahead.astype(f32) + back.astype(f32)


def scatter_sum(x, axis):
    n = lax.axis_size(axis)
    got = lax.all_to_all(x.astype(bf16), axis, split_axis=0, concat_axis=0, tiled=True)
    return jnp.sum(got.reshape(n, x.shape[0] // n, x.shape[1]).astype(f32), axis=0)


def block_units():
    places = [d for d in range(64) if (d // 8 + d % 8) % 8 < NT // 2]
    unit = [0] * 64
    for at, d in enumerate(places):
        unit[d] = at
    return unit, places


UNIT, PLACES = block_units()
COLS = 256


def scatter_kernel(place, basis, values, grad, out):
    half = pl.ds(pl.multiple_of(place[3] * 256, 256), 256)
    out[:, 0:256] = basis[0, :, half]
    out[:, 256:512] = basis[1, :, half]
    full = grad[...].astype(f32)

    def piece(d):
        block, quarter = divmod(UNIT[d], 4)
        return full[block * 8 : block * 8 + 8, quarter * COLS : (quarter + 1) * COLS]

    for d in range(0, 64, 2):
        pair = jnp.concatenate([piece(d), piece(d + 1)], axis=0)
        out[d * 8 : d * 8 + 16, 512:768] = pair.astype(bf16)
    parts, left = [], values[...]
    for _ in range(3):
        part = left.astype(bf16).astype(f32)
        parts.append(part)
        left = left - part
    rows = jnp.concatenate([*parts, jnp.zeros((122, TILE), f32)], axis=0)
    out[:, 768:896] = rows.T.astype(bf16)


def forward_kernel(owner, slot, got, out):
    found = []
    for b in range(NT):
        at = pl.multiple_of(owner[b] // 2 * 16, 16)
        pair = got[pl.ds(at, 16), :].astype(f32)
        mine = jnp.where(owner[b] % 2 == 0, pair[0:8], pair[8:16])
        rows = jnp.where(slot[b] == 0, mine[:, 0:256], mine[:, 256:512])
        found.append(jnp.concatenate([rows, mine[:, 768:896]], axis=1))
    for d in range(0, 64, 2):
        pair = jnp.concatenate([found[UNIT[d] // 4], found[UNIT[d + 1] // 4]], axis=0)
        out[d * 8 : d * 8 + 16, :] = pair.astype(bf16)


def rotate_kernel(place, mine, theirs, got, out, basis):
    core, slot = place[0], place[1]
    basis[:, pl.ds(pl.multiple_of(core * 256, 256), 256)] = mine[:, 0:256]
    basis[:, pl.ds(pl.multiple_of((1 - core) * 256, 256), 256)] = theirs[...]
    parts = mine[:, 256:384].astype(f32)
    lane = lax.broadcasted_iota(jnp.int32, parts.shape, 1)
    ours = (lane < 6) & (lane % 2 == slot)
    values = jnp.sum(jnp.where(ours, parts, 0.0), axis=1, keepdims=True)
    turned = dot(basis[...].T, got[:, 512:768])
    scaled = (turned / (values + damping)).astype(bf16)
    out[...] = dot(basis[...], scaled).astype(bf16)


def pack_kernel(total, owner, slot, first, last, rotated, out, sums, slots):
    wide = FIRST_TILES * SLAB
    for at, got in ((0, first), (wide, last)):
        full = got[...].astype(f32)
        acc = full[0:8]
        for k in range(8, full.shape[0], 8):
            acc = acc + full[k : k + 8]
        sums[:, at : at + full.shape[1]] = acc / total
    slots[...] = jnp.zeros_like(slots)
    for u in range(UT):
        row = pl.multiple_of(owner[u] * 8, 8)
        lane = pl.multiple_of(slot[u] * SLAB, SLAB)
        slots[pl.ds(row, 8), pl.ds(lane, SLAB)] = sums[:, u * SLAB : (u + 1) * SLAB]
    out[:, 0:256] = slots[...].astype(bf16)
    out[:, 256:512] = rotated[...]


def unpack_kernel(is_first, got, factor, result):
    shares = got[:, 0:256].astype(f32)
    for s in range(SLOTS):
        lanes = slice(s * SLAB, (s + 1) * SLAB)

        @pl.when(is_first[s] == 1)
        def _():
            for y in range(4):
                for x in range(2):
                    to, at = s * TILE + x * 256 + y * 64, (y * 2 + x) * 64
                    factor[to : to + 64, :] = shares[at : at + 64, lanes]

        @pl.when(is_first[s] == 0)
        def _():
            for y in range(4):
                for x in range(2):
                    for z in range(8):
                        to, at = s * TILE + z * 64 + x * 32 + y * 8, (y * 2 + x) * 64 + z * 8
                        factor[to : to + 8, :] = shares[at : at + 8, lanes]

    turned = got[:, 256:512].astype(f32)
    for b in range(0, NT, 2):
        for q in range(4):
            pair = [turned[PLACES[u] * 8 : PLACES[u] * 8 + 8] for u in (b * 4 + q, b * 4 + 4 + q)]
            result[b * 8 : b * 8 + 16, q * COLS : (q + 1) * COLS] = jnp.concatenate(pair, axis=0).astype(bf16)


def exchange(x, axis):
    return lax.all_to_all(x, axis, split_axis=0, concat_axis=0, tiled=True)


def shards(activations, tile_owner, gradient, block_owner, eigen_basis, eigen_values):
    micro, tokens, width = activations.shape
    blocks, rows, cols = gradient.shape
    dp_count = lax.axis_size(DP)
    act = activations.reshape(micro * tokens, width)
    me = lax.axis_index(DP)
    low = lax.axis_index("xl")
    high, core = lax.axis_index("xh"), lax.axis_index("c")
    place = jnp.stack([low, high * 2 + core, (1 - high) * 2 + core, core]).astype(jnp.int32)
    tile_rank = slot_rank(tile_owner).astype(jnp.int32)
    block_rank = slot_rank(block_owner).astype(jnp.int32)

    [out] = call(
        scatter_kernel, [array((TILE, 896), bf16)], [], 0,
        place, eigen_basis, eigen_values, gradient.reshape(blocks * rows, cols),
    )
    got = exchange(out, DP)

    near, far, last = sent_products(act, place)
    near = lax.ppermute(near, "xl", [(0, 1), (1, 0)])
    far = lax.ppermute(far, ("xl", "xh"), [(i, 3 - i) for i in range(4)])
    own = kept_products(act, place)

    [out] = call(forward_kernel, [array((TILE, 384), bf16)], [], 0, block_owner, block_rank, got, scalars=2)
    mine = exchange(out, DP)
    theirs = lax.ppermute(mine[:, :256], "c", [(0, 1), (1, 0)])
    my_block = jnp.asarray(np.array(UNIT) // 4, jnp.int32)[me]
    [rotated] = call(
        rotate_kernel, [array((TILE, COLS), bf16)], [((TILE, TILE), bf16)], 4 * TILE * TILE * COLS,
        jnp.stack([core, block_rank[my_block]]).astype(jnp.int32), mine, theirs, got,
    )

    last = around_z(last)
    half = last.shape[0] // 2
    sent = lax.dynamic_slice_in_dim(last, (1 - low) * half, half, 0)
    kept = lax.dynamic_slice_in_dim(last, low * half, half, 0)
    last = kept + lax.ppermute(sent.astype(bf16), "xl", [(0, 1), (1, 0)]).astype(f32)
    last = exchange(last.astype(bf16), "y")

    first = own + jnp.concatenate([near, far], axis=0).astype(f32)
    first = exchange(first.astype(bf16), "y")
    first = jnp.sum(first.reshape(4, 64, -1).astype(f32), axis=0)
    first = exchange(first.astype(bf16), "z")

    [out] = call(
        functools.partial(pack_kernel, micro * tokens * dp_count),
        [array((TILE, 512), bf16)], [((8, UT * SLAB), f32), ((TILE, 256), f32)], 0,
        tile_owner, tile_rank, first, last, rotated, scalars=2,
    )
    final = exchange(out, DP)
    slot = jnp.arange(SLOTS)
    held = (tile_owner[None, :] == me) & (tile_rank[None, :] == slot[:, None])
    is_first = jnp.any(held & (jnp.arange(UT) < FIRST_TILES)[None, :], axis=1)
    factor, result = call(
        unpack_kernel, [array((SLOTS * TILE, SLAB), f32), array((blocks * rows, cols), bf16)], [], 0,
        is_first.astype(jnp.int32), final,
    )
    return factor.reshape(SLOTS, TILE, SLAB), result.reshape(blocks, rows, cols)


def solution(mesh):
    fine = Mesh(mesh.devices.reshape(4, 2, 8, 2, 2), ("y", "xl", "z", "xh", "c"))
    group = ("xh", "c")
    placed = (
        P(None, DP, None),
        P(),
        P(None, DP, group),
        P(),
        P(DP, None, None),
        P(DP, None),
    )
    return jax.shard_map(
        shards,
        mesh=fine,
        in_specs=placed,
        out_specs=(P(DP, None, group), P(None, DP, group)),
        check_vma=False,
    )
```

```python
import functools

import jax
import jax.numpy as jnp
import numpy as np
from jax import lax
from jax.experimental import pallas as pl
from jax.experimental.pallas import tpu as pltpu
from jax.sharding import Mesh, PartitionSpec as P

TILE = 512
NT = 10
UT = NT * (NT + 1) // 2
SLOTS = 2
SLAB = 128
COLS = 256
DP = ("y", "xl", "z")
X_FIRST = (0, 1, 2, 5, 6)
Y_FIRST = tuple(i for i in range(NT) if i not in X_FIRST)
PAIRS = [(i, j) for i in range(NT) for j in range(i, NT)]
ORDER = [u for rows in (X_FIRST, Y_FIRST) for u, (i, _) in enumerate(PAIRS) if i in rows]
X_TILES = sum(NT - i for i in X_FIRST)
Y_TILES = UT - X_TILES

damping = 0.1
bf16 = jnp.bfloat16
f32 = jnp.float32


def slot_rank(owner_ids):
    entries = owner_ids.shape[0]
    position = jnp.arange(entries)
    same_owner = owner_ids[:, None] == owner_ids[None, :]
    earlier = position[None, :] < position[:, None]
    return jnp.sum(jnp.logical_and(same_owner, earlier), axis=1)


def dot(a, b):
    return lax.dot_general(a, b, (((1,), (0,)), ((), ())), preferred_element_type=f32)


def fill(slab, act, which, begin):
    for j in range(begin, NT):
        at = pl.multiple_of(j * TILE + which * SLAB, SLAB)
        slab[:, j * SLAB : (j + 1) * SLAB] = act[:, pl.ds(at, SLAB)]


def spans(i):
    return [(at, min(at + 256, NT * SLAB)) for at in range(i * SLAB, NT * SLAB, 256)]


def turn(act, i, y, turned, half=None):
    part = turned.shape[0] // 4
    for k in range(4):
        at = pl.multiple_of(i * TILE + lax.rem(y + k, 4) * SLAB, SLAB)
        chunk = act[:, pl.ds(at, SLAB)].T
        if half is not None:
            chunk = jnp.where(half == 0, chunk[:part], chunk[part:])
        turned[k * part : (k + 1) * part, :] = chunk


def sent_kernel(place, act, near, far, slab, other, turned):
    low, mine, theirs, y = place[0], place[1], place[2], place[3]
    fill(slab, act, mine, 0)
    fill(other, act, theirs, 0)
    start = 0
    for i in X_FIRST:
        turn(act, i, y, turned, 1 - low)
        for begin, end in spans(i):
            to = slice(start, start + end - begin)
            near[:, to] = dot(turned[0:128, :], slab[:, begin:end]).astype(bf16)
            far[:, to] = dot(turned[128:256, :], other[:, begin:end]).astype(bf16)
            start += end - begin


def kept_kernel(place, act, own0, own1, own2, own3, slab, turned):
    low, mine, y = place[0], place[1], place[3]
    fill(slab, act, mine, 0)
    start = 0
    for i in X_FIRST:
        turn(act, i, y, turned, low)
        for begin, end in spans(i):
            product = dot(turned[...], slab[:, begin:end])
            for k, own in enumerate((own0, own1, own2, own3)):
                own[:, start : start + end - begin] = product[k * 64 : k * 64 + 64]
            start += end - begin


def along_kernel(place, act, own0, own1, up, down, own3, slab, turned):
    mine, y = place[1], place[3]
    fill(slab, act, mine, min(Y_FIRST))
    start = 0
    for i in Y_FIRST:
        turn(act, i, y, turned)
        for begin, end in spans(i):
            to = slice(start, start + end - begin)
            product = dot(turned[...], slab[:, begin:end])
            own0[:, to] = product[0:128]
            own1[:, to] = product[128:256]
            up[:, to] = product[256:320].astype(bf16)
            down[:, to] = product[320:384].astype(bf16)
            own3[:, to] = product[384:512]
            start += end - begin


VMEM = pl.BlockSpec(memory_space=pltpu.VMEM)
SMEM = pl.BlockSpec(memory_space=pltpu.SMEM)


def call(kernel, outs, scratch, flops, *operands, scalars=1):
    moved = sum(x.size * x.dtype.itemsize for x in operands)
    moved += sum(x.size * x.dtype.itemsize for x in outs)
    return pl.pallas_call(
        kernel,
        out_shape=tuple(outs),
        in_specs=[SMEM] * scalars + [VMEM] * (len(operands) - scalars),
        out_specs=(VMEM,) * len(outs),
        scratch_shapes=[pltpu.VMEM(shape, dtype) for shape, dtype in scratch],
        compiler_params=pltpu.CompilerParams(vmem_limit_bytes=40 * 2**20),
        cost_estimate=pl.CostEstimate(flops=flops, bytes_accessed=moved, transcendentals=0),
    )(*operands)


def array(shape, dtype):
    return jax.ShapeDtypeStruct(shape, dtype)


def products(act, place):
    tokens = act.shape[0]
    wide, rest = X_TILES * SLAB, Y_TILES * SLAB
    slab = ((tokens, NT * SLAB), bf16)
    half = ((256, tokens), bf16)
    full = ((TILE, tokens), bf16)
    sent = call(
        sent_kernel, [array((128, wide), bf16)] * 2, [slab, slab, half], 2 * tokens * 256 * wide, place, act
    )
    along = call(
        along_kernel,
        [array((128, rest), f32)] * 2 + [array((64, rest), bf16)] * 2 + [array((128, rest), f32)],
        [slab, full],
        2 * tokens * TILE * rest,
        place,
        act,
    )
    kept = call(kept_kernel, [array((64, wide), f32)] * 4, [slab, half], 2 * tokens * 256 * wide, place, act)
    return sent, along, kept


def ring(axis, step):
    n = lax.axis_size(axis)
    return [(i, (i + step) % n) for i in range(n)]


def around_y(zero, one, up, down, three):
    up = lax.ppermute(up, "y", ring("y", 1))
    down = lax.ppermute(down, "y", ring("y", -1))
    none = jnp.zeros_like(up)
    up = one() + jnp.concatenate([up, none], axis=0).astype(f32)
    down = three() + jnp.concatenate([none, down], axis=0).astype(f32)
    up = lax.ppermute(up.astype(bf16), "y", ring("y", 1))
    down = lax.ppermute(down.astype(bf16), "y", ring("y", -1))
    return zero() + up.astype(f32) + down.astype(f32)


def block_units():
    places = [d for d in range(64) if (d // 8 + d % 8) % 8 < NT // 2]
    unit = [0] * 64
    for at, d in enumerate(places):
        unit[d] = at
    return unit, places


UNIT, PLACES = block_units()


def scatter_kernel(place, basis, values, grad, out):
    quarter = pl.ds(pl.multiple_of(place[1] * SLAB, SLAB), SLAB)
    out[:, 0:128] = basis[0, :, quarter]
    out[:, 128:256] = basis[1, :, quarter]
    full = grad[...].astype(f32)

    def piece(d):
        block, part = divmod(UNIT[d], 4)
        return full[block * 8 : block * 8 + 8, part * COLS : (part + 1) * COLS]

    for d in range(0, 64, 2):
        pair = jnp.concatenate([piece(d), piece(d + 1)], axis=0)
        out[d * 8 : d * 8 + 16, 256:512] = pair.astype(bf16)
    parts, left = [], values[...]
    for _ in range(3):
        part = left.astype(bf16).astype(f32)
        parts.append(part)
        left = left - part
    rows = jnp.concatenate([*parts, jnp.zeros((122, TILE), f32)], axis=0)
    out[:, 512:640] = rows.T.astype(bf16)


def forward_kernel(owner, slot, got, out):
    found = []
    for b in range(NT):
        at = pl.multiple_of(owner[b] // 2 * 16, 16)
        pair = got[pl.ds(at, 16), :].astype(f32)
        mine = jnp.where(owner[b] % 2 == 0, pair[0:8], pair[8:16])
        rows = jnp.where(slot[b] == 0, mine[:, 0:128], mine[:, 128:256])
        found.append(jnp.concatenate([rows, mine[:, 512:640]], axis=1))
    for d in range(0, 64, 2):
        pair = jnp.concatenate([found[UNIT[d] // 4], found[UNIT[d + 1] // 4]], axis=0)
        out[d * 8 : d * 8 + 16, :] = pair.astype(bf16)


def rotate_kernel(place, mine, one, two, three, got, out, basis):
    group, slot = place[0], place[1]
    for k, quarter in enumerate((mine, one, two, three)):
        at = pl.multiple_of(lax.bitwise_xor(group, k) * SLAB, SLAB)
        basis[:, pl.ds(at, SLAB)] = quarter[:, 0:128]
    parts = mine[:, 128:256].astype(f32)
    lane = lax.broadcasted_iota(jnp.int32, parts.shape, 1)
    ours = (lane < 6) & (lane % 2 == slot)
    values = jnp.sum(jnp.where(ours, parts, 0.0), axis=1, keepdims=True)
    turned = dot(basis[...].T, got[:, 256:512])
    scaled = (turned / (values + damping)).astype(bf16)
    out[...] = dot(basis[...], scaled).astype(bf16)


def pack_kernel(total, owner, slot, got, out, sums, slots):
    full = got[...].astype(f32)
    acc = full[0:8]
    for k in range(8, 64, 8):
        acc = acc + full[k : k + 8]
    sums[...] = acc / total
    slots[...] = jnp.zeros_like(slots)
    for at, u in enumerate(ORDER):
        row = pl.multiple_of(owner[u] * 8, 8)
        lane = pl.multiple_of(slot[u] * SLAB, SLAB)
        slots[pl.ds(row, 8), pl.ds(lane, SLAB)] = sums[:, at * SLAB : (at + 1) * SLAB]
    out[...] = slots[...].astype(bf16)


def unpack_kernel(got, returned, factor, result):
    for s in range(SLOTS):
        factor[s * TILE : (s + 1) * TILE, :] = got[:, s * SLAB : (s + 1) * SLAB].astype(f32)
    turned = returned[...].astype(f32)
    for b in range(0, NT, 2):
        for q in range(4):
            pair = [turned[PLACES[u] * 8 : PLACES[u] * 8 + 8] for u in (b * 4 + q, b * 4 + 4 + q)]
            result[b * 8 : b * 8 + 16, q * COLS : (q + 1) * COLS] = jnp.concatenate(pair, axis=0).astype(bf16)


def exchange(x, axis):
    return lax.all_to_all(x, axis, split_axis=0, concat_axis=0, tiled=True)


def shards(activations, tile_owner, gradient, block_owner, eigen_basis, eigen_values):
    micro, tokens, width = activations.shape
    blocks, rows, cols = gradient.shape
    dp_count = lax.axis_size(DP)
    act = activations.reshape(micro * tokens, width)
    me = lax.axis_index(DP)
    y, low = lax.axis_index("y"), lax.axis_index("xl")
    high, core = lax.axis_index("xh"), lax.axis_index("c")
    group = high * 2 + core
    place = jnp.stack([low, group, (1 - high) * 2 + core, y]).astype(jnp.int32)
    tile_rank = slot_rank(tile_owner).astype(jnp.int32)
    block_rank = slot_rank(block_owner).astype(jnp.int32)

    (near, far), (zero, one, up, down, three), own = products(act, place)
    near = lax.ppermute(near, "xl", [(0, 1), (1, 0)])
    far = lax.ppermute(far, ("xl", "xh"), [(i, 3 - i) for i in range(4)])

    [out] = call(
        scatter_kernel, [array((TILE, 640), bf16)], [], 0,
        place, eigen_basis, eigen_values, gradient.reshape(blocks * rows, cols),
    )
    got = exchange(out, DP)
    [out] = call(forward_kernel, [array((TILE, 256), bf16)], [], 0, block_owner, block_rank, got, scalars=2)
    mine = exchange(out, DP)
    quarter = mine[:, :SLAB]
    others = [lax.ppermute(quarter, ("xh", "c"), [(i, i ^ k) for i in range(4)]) for k in (1, 2, 3)]
    my_block = jnp.asarray(np.array(UNIT) // 4, jnp.int32)[me]
    [rotated] = call(
        rotate_kernel, [array((TILE, COLS), bf16)], [((TILE, TILE), bf16)], 4 * TILE * TILE * COLS,
        jnp.stack([group, block_rank[my_block]]).astype(jnp.int32), mine, *others, got,
    )
    returned = exchange(rotated, DP)

    along = around_y(lambda: zero, lambda: one, up, down, lambda: three)
    half = along.shape[0] // 2
    sent = lax.dynamic_slice_in_dim(along, (1 - low) * half, half, 0)
    kept = lax.dynamic_slice_in_dim(along, low * half, half, 0)
    along = kept + lax.ppermute(sent.astype(bf16), "xl", [(0, 1), (1, 0)]).astype(f32)

    opposite = (own[2] + far[:64].astype(f32)).astype(bf16)
    across = around_y(
        lambda: own[0] + near[:64].astype(f32),
        lambda: own[1] + near[64:].astype(f32),
        opposite[:32],
        opposite[32:],
        lambda: own[3] + far[64:].astype(f32),
    )
    sums = exchange(jnp.concatenate([across.astype(bf16), along.astype(bf16)], axis=1), "z")

    [out] = call(
        functools.partial(pack_kernel, micro * tokens * dp_count),
        [array((TILE, 256), bf16)], [((8, UT * SLAB), f32), ((TILE, 256), f32)], 0,
        tile_owner, tile_rank, sums, scalars=2,
    )
    final = exchange(out, DP)
    factor, result = call(
        unpack_kernel, [array((SLOTS * TILE, SLAB), f32), array((blocks * rows, cols), bf16)], [], 0,
        final, returned, scalars=0,
    )
    return factor.reshape(SLOTS, TILE, SLAB), result.reshape(blocks, rows, cols)


def solution(mesh):
    fine = Mesh(mesh.devices.reshape(4, 2, 8, 2, 2), ("y", "xl", "z", "xh", "c"))
    group = ("xh", "c")
    placed = (
        P(None, DP, None),
        P(),
        P(None, DP, group),
        P(),
        P(DP, None, None),
        P(DP, None),
    )
    return jax.shard_map(
        shards,
        mesh=fine,
        in_specs=placed,
        out_specs=(P(DP, None, group), P(None, DP, group)),
        check_vma=False,
    )
```

```python
import functools

import jax
import jax.numpy as jnp
import numpy as np
from jax import lax
from jax.experimental import pallas as pl
from jax.experimental.pallas import tpu as pltpu
from jax.sharding import Mesh, PartitionSpec as P

TILE = 512
NT = 10
UT = NT * (NT + 1) // 2
SLOTS = 2
SLAB = 128
COLS = 256
DP = ("y", "xl", "z")
X_FIRST = (0, 1, 2, 5, 6)
Y_FIRST = tuple(i for i in range(NT) if i not in X_FIRST)
PAIRS = [(i, j) for i in range(NT) for j in range(i, NT)]
ORDER = [u for rows in (X_FIRST, Y_FIRST) for u, (i, _) in enumerate(PAIRS) if i in rows]
X_TILES = sum(NT - i for i in X_FIRST)
Y_TILES = UT - X_TILES

damping = 0.1
bf16 = jnp.bfloat16
f32 = jnp.float32


def slot_rank(owner_ids):
    entries = owner_ids.shape[0]
    position = jnp.arange(entries)
    same_owner = owner_ids[:, None] == owner_ids[None, :]
    earlier = position[None, :] < position[:, None]
    return jnp.sum(jnp.logical_and(same_owner, earlier), axis=1)


def dot(a, b):
    return lax.dot_general(a, b, (((1,), (0,)), ((), ())), preferred_element_type=f32)


def fill(slab, act, which, begin):
    for j in range(begin, NT):
        at = pl.multiple_of(j * TILE + which * SLAB, SLAB)
        slab[:, j * SLAB : (j + 1) * SLAB] = act[:, pl.ds(at, SLAB)]


def spans(i):
    return [(at, min(at + 256, NT * SLAB)) for at in range(i * SLAB, NT * SLAB, 256)]


def turn(act, i, y, turned, half=None):
    part = turned.shape[0] // 4
    for k in range(4):
        at = pl.multiple_of(i * TILE + lax.rem(y + k, 4) * SLAB, SLAB)
        chunk = act[:, pl.ds(at, SLAB)].T
        if half is not None:
            chunk = jnp.where(half == 0, chunk[:part], chunk[part:])
        turned[k * part : (k + 1) * part, :] = chunk


def sent_kernel(place, act, near, far, slab, other, turned):
    low, mine, theirs, y = place[0], place[1], place[2], place[3]
    fill(slab, act, mine, 0)
    fill(other, act, theirs, 0)
    start = 0
    for i in X_FIRST:
        turn(act, i, y, turned, 1 - low)
        for begin, end in spans(i):
            to = slice(start, start + end - begin)
            near[:, to] = dot(turned[0:128, :], slab[:, begin:end]).astype(bf16)
            far[:, to] = dot(turned[128:256, :], other[:, begin:end]).astype(bf16)
            start += end - begin


def kept_kernel(place, act, own0, own1, own2, own3, slab, turned):
    low, mine, y = place[0], place[1], place[3]
    fill(slab, act, mine, 0)
    start = 0
    for i in X_FIRST:
        turn(act, i, y, turned, low)
        for begin, end in spans(i):
            product = dot(turned[...], slab[:, begin:end])
            for k, own in enumerate((own0, own1, own2, own3)):
                own[:, start : start + end - begin] = product[k * 64 : k * 64 + 64]
            start += end - begin


def along_kernel(place, act, own0, own1, up, down, own3, slab, turned):
    mine, y = place[1], place[3]
    fill(slab, act, mine, min(Y_FIRST))
    start = 0
    for i in Y_FIRST:
        turn(act, i, y, turned)
        for begin, end in spans(i):
            to = slice(start, start + end - begin)
            product = dot(turned[...], slab[:, begin:end])
            own0[:, to] = product[0:128]
            own1[:, to] = product[128:256]
            up[:, to] = product[256:320].astype(bf16)
            down[:, to] = product[320:384].astype(bf16)
            own3[:, to] = product[384:512]
            start += end - begin


VMEM = pl.BlockSpec(memory_space=pltpu.VMEM)
SMEM = pl.BlockSpec(memory_space=pltpu.SMEM)


def call(kernel, outs, scratch, flops, *operands, scalars=1, after=(), vmem=12):
    moved = sum(x.size * x.dtype.itemsize for x in operands)
    moved += sum(x.size * x.dtype.itemsize for x in outs)
    count = len(operands)

    def body(*refs):
        kernel(*refs[:count], *refs[count + len(after) :])

    return pl.pallas_call(
        body,
        out_shape=tuple(outs),
        in_specs=[SMEM] * scalars + [VMEM] * (count - scalars) + [pl.BlockSpec(memory_space=pl.ANY)] * len(after),
        out_specs=(VMEM,) * len(outs),
        scratch_shapes=[pltpu.VMEM(shape, dtype) for shape, dtype in scratch],
        compiler_params=pltpu.CompilerParams(vmem_limit_bytes=vmem * 2**20),
        cost_estimate=pl.CostEstimate(flops=flops, bytes_accessed=moved, transcendentals=0),
    )(*operands, *after)


def array(shape, dtype):
    return jax.ShapeDtypeStruct(shape, dtype)


def sent_products(act, place):
    tokens = act.shape[0]
    wide = X_TILES * SLAB
    slab, half = ((tokens, NT * SLAB), bf16), ((256, tokens), bf16)
    return call(sent_kernel, [array((128, wide), bf16)] * 2, [slab, slab, half], 2 * tokens * 256 * wide, place, act)


def kept_products(act, place, after):
    tokens = act.shape[0]
    wide = X_TILES * SLAB
    slab, half = ((tokens, NT * SLAB), bf16), ((256, tokens), bf16)
    outs = [array((64, wide), f32)] * 4
    return call(kept_kernel, outs, [slab, half], 2 * tokens * 256 * wide, place, act, after=after)


def along_products(act, place, after):
    tokens = act.shape[0]
    wide = Y_TILES * SLAB
    slab, full = ((tokens, NT * SLAB), bf16), ((TILE, tokens), bf16)
    outs = [array((128, wide), f32)] * 2 + [array((64, wide), bf16)] * 2 + [array((128, wide), f32)]
    return call(along_kernel, outs, [slab, full], 2 * tokens * TILE * wide, place, act, after=after)


def ring(axis, step):
    n = lax.axis_size(axis)
    return [(i, (i + step) % n) for i in range(n)]


def around_y(zero, one, up, down, three):
    up = lax.ppermute(up, "y", ring("y", 1))
    down = lax.ppermute(down, "y", ring("y", -1))
    none = jnp.zeros_like(up)
    up = one() + jnp.concatenate([up, none], axis=0).astype(f32)
    down = three() + jnp.concatenate([none, down], axis=0).astype(f32)
    up = lax.ppermute(up.astype(bf16), "y", ring("y", 1))
    down = lax.ppermute(down.astype(bf16), "y", ring("y", -1))
    return zero() + up.astype(f32) + down.astype(f32)


def block_units():
    places = [d for d in range(64) if (d // 8 + d % 8) % 8 < NT // 2]
    unit = [0] * 64
    for at, d in enumerate(places):
        unit[d] = at
    return unit, places


UNIT, PLACES = block_units()


def scatter_kernel(place, basis, values, grad, out):
    quarter = pl.ds(pl.multiple_of(place[1] * SLAB, SLAB), SLAB)
    out[:, 0:128] = basis[0, :, quarter]
    out[:, 128:256] = basis[1, :, quarter]
    full = grad[...].astype(f32)

    def piece(d):
        block, part = divmod(UNIT[d], 4)
        return full[block * 8 : block * 8 + 8, part * COLS : (part + 1) * COLS]

    for d in range(0, 64, 2):
        pair = jnp.concatenate([piece(d), piece(d + 1)], axis=0)
        out[d * 8 : d * 8 + 16, 256:512] = pair.astype(bf16)
    parts, left = [], values[...]
    for _ in range(3):
        part = left.astype(bf16).astype(f32)
        parts.append(part)
        left = left - part
    rows = jnp.concatenate([*parts, jnp.zeros((122, TILE), f32)], axis=0)
    out[:, 512:640] = rows.T.astype(bf16)


def forward_kernel(owner, slot, got, out):
    found = []
    for b in range(NT):
        at = pl.multiple_of(owner[b] // 2 * 16, 16)
        pair = got[pl.ds(at, 16), :].astype(f32)
        mine = jnp.where(owner[b] % 2 == 0, pair[0:8], pair[8:16])
        rows = jnp.where(slot[b] == 0, mine[:, 0:128], mine[:, 128:256])
        found.append(jnp.concatenate([rows, mine[:, 512:640]], axis=1))
    for d in range(0, 64, 2):
        pair = jnp.concatenate([found[UNIT[d] // 4], found[UNIT[d + 1] // 4]], axis=0)
        out[d * 8 : d * 8 + 16, :] = pair.astype(bf16)


def rotate_kernel(place, mine, one, two, three, got, out, basis):
    group, slot = place[0], place[1]
    for k, quarter in enumerate((mine, one, two, three)):
        at = pl.multiple_of(lax.bitwise_xor(group, k) * SLAB, SLAB)
        basis[:, pl.ds(at, SLAB)] = quarter[:, 0:128]
    parts = mine[:, 128:256].astype(f32)
    lane = lax.broadcasted_iota(jnp.int32, parts.shape, 1)
    ours = (lane < 6) & (lane % 2 == slot)
    values = jnp.sum(jnp.where(ours, parts, 0.0), axis=1, keepdims=True)
    turned = dot(basis[...].T, got[:, 256:512])
    scaled = (turned / (values + damping)).astype(bf16)
    out[...] = dot(basis[...], scaled).astype(bf16)


def pack_kernel(total, owner, slot, got, rotated, out, sums, slots):
    full = got[...].astype(f32)
    acc = full[0:8]
    for k in range(8, 64, 8):
        acc = acc + full[k : k + 8]
    sums[...] = acc / total
    slots[...] = jnp.zeros_like(slots)
    for at, u in enumerate(ORDER):
        row = pl.multiple_of(owner[u] * 8, 8)
        lane = pl.multiple_of(slot[u] * SLAB, SLAB)
        slots[pl.ds(row, 8), pl.ds(lane, SLAB)] = sums[:, at * SLAB : (at + 1) * SLAB]
    out[:, 0:256] = slots[...].astype(bf16)
    out[:, 256:512] = rotated[...]


def unpack_kernel(got, factor, result):
    for s in range(SLOTS):
        factor[s * TILE : (s + 1) * TILE, :] = got[:, s * SLAB : (s + 1) * SLAB].astype(f32)
    turned = got[:, 256:512].astype(f32)
    for b in range(0, NT, 2):
        for q in range(4):
            pair = [turned[PLACES[u] * 8 : PLACES[u] * 8 + 8] for u in (b * 4 + q, b * 4 + 4 + q)]
            result[b * 8 : b * 8 + 16, q * COLS : (q + 1) * COLS] = jnp.concatenate(pair, axis=0).astype(bf16)


def exchange(x, axis):
    return lax.all_to_all(x, axis, split_axis=0, concat_axis=0, tiled=True)


def shards(activations, tile_owner, gradient, block_owner, eigen_basis, eigen_values):
    micro, tokens, width = activations.shape
    blocks, rows, cols = gradient.shape
    dp_count = lax.axis_size(DP)
    act = activations.reshape(micro * tokens, width)
    me = lax.axis_index(DP)
    y, low = lax.axis_index("y"), lax.axis_index("xl")
    high, core = lax.axis_index("xh"), lax.axis_index("c")
    group = high * 2 + core
    place = jnp.stack([low, group, (1 - high) * 2 + core, y]).astype(jnp.int32)
    tile_rank = slot_rank(tile_owner).astype(jnp.int32)
    block_rank = slot_rank(block_owner).astype(jnp.int32)

    near, far = sent_products(act, place)
    zero, one, up, down, three = along_products(act, place, (near,))
    near = lax.ppermute(near, "xl", [(0, 1), (1, 0)])
    far = lax.ppermute(far, ("xl", "xh"), [(i, 3 - i) for i in range(4)])

    [out] = call(
        scatter_kernel, [array((TILE, 640), bf16)], [], 0,
        place, eigen_basis, eigen_values, gradient.reshape(blocks * rows, cols), after=(up,),
    )
    own = kept_products(act, place, (out,))
    got = exchange(out, DP)
    [out] = call(
        forward_kernel, [array((TILE, 256), bf16)], [], 0,
        block_owner, block_rank, got, scalars=2, after=(near, far),
    )
    mine = exchange(out, DP)
    quarter = mine[:, :SLAB]
    others = [lax.ppermute(quarter, ("xh", "c"), [(i, i ^ k) for i in range(4)]) for k in (1, 2, 3)]
    my_block = jnp.asarray(np.array(UNIT) // 4, jnp.int32)[me]
    [rotated] = call(
        rotate_kernel, [array((TILE, COLS), bf16)], [((TILE, TILE), bf16)], 4 * TILE * TILE * COLS,
        jnp.stack([group, block_rank[my_block]]).astype(jnp.int32), mine, *others, got,
    )

    along = around_y(lambda: zero, lambda: one, up, down, lambda: three)
    half = along.shape[0] // 2
    sent = lax.dynamic_slice_in_dim(along, (1 - low) * half, half, 0)
    kept = lax.dynamic_slice_in_dim(along, low * half, half, 0)
    along = kept + lax.ppermute(sent.astype(bf16), "xl", [(0, 1), (1, 0)]).astype(f32)

    opposite = (own[2] + far[:64].astype(f32)).astype(bf16)
    across = around_y(
        lambda: own[0] + near[:64].astype(f32),
        lambda: own[1] + near[64:].astype(f32),
        opposite[:32],
        opposite[32:],
        lambda: own[3] + far[64:].astype(f32),
    )
    sums = exchange(jnp.concatenate([across.astype(bf16), along.astype(bf16)], axis=1), "z")

    [out] = call(
        functools.partial(pack_kernel, micro * tokens * dp_count),
        [array((TILE, 512), bf16)], [((8, UT * SLAB), f32), ((TILE, 256), f32)], 0,
        tile_owner, tile_rank, sums, rotated, scalars=2,
    )
    final = exchange(out, DP)
    factor, result = call(
        unpack_kernel, [array((SLOTS * TILE, SLAB), f32), array((blocks * rows, cols), bf16)], [], 0,
        final, scalars=0,
    )
    return factor.reshape(SLOTS, TILE, SLAB), result.reshape(blocks, rows, cols)


def solution(mesh):
    fine = Mesh(mesh.devices.reshape(4, 2, 8, 2, 2), ("y", "xl", "z", "xh", "c"))
    group = ("xh", "c")
    placed = (
        P(None, DP, None),
        P(),
        P(None, DP, group),
        P(),
        P(DP, None, None),
        P(DP, None),
    )
    return jax.shard_map(
        shards,
        mesh=fine,
        in_specs=placed,
        out_specs=(P(DP, None, group), P(None, DP, group)),
        check_vma=False,
    )
```

```python
import functools

import jax
import jax.numpy as jnp
import numpy as np
from jax import lax
from jax.experimental import pallas as pl
from jax.experimental.pallas import tpu as pltpu
from jax.sharding import Mesh, PartitionSpec as P

TILE = 512
NT = 10
UT = NT * (NT + 1) // 2
SLOTS = 2
SLAB = 128
COLS = 256
DP = ("y", "xl", "z")
X_FIRST = (0, 1, 2, 5, 6)
Y_FIRST = tuple(i for i in range(NT) if i not in X_FIRST)
PAIRS = [(i, j) for i in range(NT) for j in range(i, NT)]
ORDER = [u for rows in (X_FIRST, Y_FIRST) for u, (i, _) in enumerate(PAIRS) if i in rows]
X_TILES = sum(NT - i for i in X_FIRST)
Y_TILES = UT - X_TILES

damping = 0.1
bf16 = jnp.bfloat16
f32 = jnp.float32


def slot_rank(owner_ids):
    entries = owner_ids.shape[0]
    position = jnp.arange(entries)
    same_owner = owner_ids[:, None] == owner_ids[None, :]
    earlier = position[None, :] < position[:, None]
    return jnp.sum(jnp.logical_and(same_owner, earlier), axis=1)


def dot(a, b):
    return lax.dot_general(a, b, (((1,), (0,)), ((), ())), preferred_element_type=f32)


def fill(slab, act, which, begin):
    for j in range(begin, NT):
        at = pl.multiple_of(j * TILE + which * SLAB, SLAB)
        slab[:, j * SLAB : (j + 1) * SLAB] = act[:, pl.ds(at, SLAB)]


def spans(i):
    return [(at, min(at + 256, NT * SLAB)) for at in range(i * SLAB, NT * SLAB, 256)]


def turn(act, i, y, turned, half=None):
    part = turned.shape[0] // 4
    for k in range(4):
        at = pl.multiple_of(i * TILE + lax.rem(y + k, 4) * SLAB, SLAB)
        chunk = act[:, pl.ds(at, SLAB)].T
        if half is not None:
            chunk = jnp.where(half == 0, chunk[:part], chunk[part:])
        turned[k * part : (k + 1) * part, :] = chunk


def sent_kernel(place, act, near, far, slab, other, turned):
    low, mine, theirs, y = place[0], place[1], place[2], place[3]
    fill(slab, act, mine, 0)
    fill(other, act, theirs, 0)
    start = 0
    for i in X_FIRST:
        turn(act, i, y, turned, 1 - low)
        for begin, end in spans(i):
            to = slice(start, start + end - begin)
            near[:, to] = dot(turned[0:128, :], slab[:, begin:end]).astype(bf16)
            far[:, to] = dot(turned[128:256, :], other[:, begin:end]).astype(bf16)
            start += end - begin


def kept_kernel(place, act, own0, own1, own2, own3, slab, turned):
    low, mine, y = place[0], place[1], place[3]
    fill(slab, act, mine, 0)
    start = 0
    for i in X_FIRST:
        turn(act, i, y, turned, low)
        for begin, end in spans(i):
            product = dot(turned[...], slab[:, begin:end])
            for k, own in enumerate((own0, own1, own2, own3)):
                own[:, start : start + end - begin] = product[k * 64 : k * 64 + 64]
            start += end - begin


def along_kernel(place, act, own0, own1, up, down, own3, slab, turned):
    mine, y = place[1], place[3]
    fill(slab, act, mine, min(Y_FIRST))
    start = 0
    for i in Y_FIRST:
        turn(act, i, y, turned)
        for begin, end in spans(i):
            to = slice(start, start + end - begin)
            product = dot(turned[...], slab[:, begin:end])
            own0[:, to] = product[0:128]
            own1[:, to] = product[128:256]
            up[:, to] = product[256:320].astype(bf16)
            down[:, to] = product[320:384].astype(bf16)
            own3[:, to] = product[384:512]
            start += end - begin


VMEM = pl.BlockSpec(memory_space=pltpu.VMEM)
SMEM = pl.BlockSpec(memory_space=pltpu.SMEM)


def call(kernel, outs, scratch, flops, *operands, scalars=1, after=(), vmem=12):
    moved = sum(x.size * x.dtype.itemsize for x in operands)
    moved += sum(x.size * x.dtype.itemsize for x in outs)
    count = len(operands)

    def body(*refs):
        kernel(*refs[:count], *refs[count + len(after) :])

    return pl.pallas_call(
        body,
        out_shape=tuple(outs),
        in_specs=[SMEM] * scalars + [VMEM] * (count - scalars) + [pl.BlockSpec(memory_space=pl.ANY)] * len(after),
        out_specs=(VMEM,) * len(outs),
        scratch_shapes=[pltpu.VMEM(shape, dtype) for shape, dtype in scratch],
        compiler_params=pltpu.CompilerParams(vmem_limit_bytes=vmem * 2**20),
        cost_estimate=pl.CostEstimate(flops=flops, bytes_accessed=moved, transcendentals=0),
    )(*operands, *after)


def array(shape, dtype):
    return jax.ShapeDtypeStruct(shape, dtype)


def sent_products(act, place):
    tokens = act.shape[0]
    wide = X_TILES * SLAB
    slab, half = ((tokens, NT * SLAB), bf16), ((256, tokens), bf16)
    return call(sent_kernel, [array((128, wide), bf16)] * 2, [slab, slab, half], 2 * tokens * 256 * wide, place, act)


def kept_products(act, place, after):
    tokens = act.shape[0]
    wide = X_TILES * SLAB
    slab, half = ((tokens, NT * SLAB), bf16), ((256, tokens), bf16)
    outs = [array((64, wide), f32)] * 4
    return call(kept_kernel, outs, [slab, half], 2 * tokens * 256 * wide, place, act, after=after)


def along_products(act, place, after):
    tokens = act.shape[0]
    wide = Y_TILES * SLAB
    slab, full = ((tokens, NT * SLAB), bf16), ((TILE, tokens), bf16)
    outs = [array((128, wide), f32)] * 2 + [array((64, wide), bf16)] * 2 + [array((128, wide), f32)]
    return call(along_kernel, outs, [slab, full], 2 * tokens * TILE * wide, place, act, after=after)


def ring(axis, step):
    n = lax.axis_size(axis)
    return [(i, (i + step) % n) for i in range(n)]


def around_y(zero, one, up, down, three):
    up = lax.ppermute(up, "y", ring("y", 1))
    down = lax.ppermute(down, "y", ring("y", -1))
    none = jnp.zeros_like(up)
    up = one() + jnp.concatenate([up, none], axis=0).astype(f32)
    down = three() + jnp.concatenate([none, down], axis=0).astype(f32)
    up = lax.ppermute(up.astype(bf16), "y", ring("y", 1))
    down = lax.ppermute(down.astype(bf16), "y", ring("y", -1))
    return zero() + up.astype(f32) + down.astype(f32)


def block_units():
    places = [d for d in range(64) if (d // 8 + d % 8) % 8 < NT // 2]
    unit = [0] * 64
    for at, d in enumerate(places):
        unit[d] = at
    return unit, places


UNIT, PLACES = block_units()


def scatter_kernel(place, basis, values, grad, out):
    quarter = pl.ds(pl.multiple_of(place[1] * SLAB, SLAB), SLAB)
    out[:, 0:128] = basis[0, :, quarter]
    out[:, 128:256] = basis[1, :, quarter]
    full = grad[...].astype(f32)

    def piece(d):
        block, part = divmod(UNIT[d], 4)
        return full[block * 8 : block * 8 + 8, part * COLS : (part + 1) * COLS]

    for d in range(0, 64, 2):
        pair = jnp.concatenate([piece(d), piece(d + 1)], axis=0)
        out[d * 8 : d * 8 + 16, 256:512] = pair.astype(bf16)
    parts, left = [], values[...]
    for _ in range(3):
        part = left.astype(bf16).astype(f32)
        parts.append(part)
        left = left - part
    rows = jnp.concatenate([*parts, jnp.zeros((122, TILE), f32)], axis=0)
    out[:, 512:640] = rows.T.astype(bf16)


def forward_kernel(owner, slot, got, out):
    found = []
    for b in range(NT):
        at = pl.multiple_of(owner[b] // 2 * 16, 16)
        pair = got[pl.ds(at, 16), :].astype(f32)
        mine = jnp.where(owner[b] % 2 == 0, pair[0:8], pair[8:16])
        rows = jnp.where(slot[b] == 0, mine[:, 0:128], mine[:, 128:256])
        found.append(jnp.concatenate([rows, mine[:, 512:640]], axis=1))
    for d in range(0, 64, 2):
        pair = jnp.concatenate([found[UNIT[d] // 4], found[UNIT[d + 1] // 4]], axis=0)
        out[d * 8 : d * 8 + 16, :] = pair.astype(bf16)


def rotate_kernel(place, mine, one, two, three, got, out, basis):
    group, slot = place[0], place[1]
    for k, quarter in enumerate((mine, one, two, three)):
        at = pl.multiple_of(lax.bitwise_xor(group, k) * SLAB, SLAB)
        basis[:, pl.ds(at, SLAB)] = quarter[:, 0:128]
    parts = mine[:, 128:256].astype(f32)
    lane = lax.broadcasted_iota(jnp.int32, parts.shape, 1)
    ours = (lane < 6) & (lane % 2 == slot)
    values = jnp.sum(jnp.where(ours, parts, 0.0), axis=1, keepdims=True)
    turned = dot(basis[...].T, got[:, 256:512])
    scaled = (turned / (values + damping)).astype(bf16)
    out[...] = dot(basis[...], scaled).astype(bf16)


def pack_kernel(total, owner, slot, got, rotated, out, sums, slots):
    full = got[...].astype(f32)
    acc = full[0:8]
    for k in range(8, 64, 8):
        acc = acc + full[k : k + 8]
    sums[...] = acc / total
    slots[...] = jnp.zeros_like(slots)
    for at, u in enumerate(ORDER):
        row = pl.multiple_of(owner[u] * 8, 8)
        lane = pl.multiple_of(slot[u] * SLAB, SLAB)
        slots[pl.ds(row, 8), pl.ds(lane, SLAB)] = sums[:, at * SLAB : (at + 1) * SLAB]
    out[:, 0:256] = slots[...].astype(bf16)
    out[:, 256:512] = rotated[...]


def unpack_kernel(got, factor, result):
    for s in range(SLOTS):
        factor[s * TILE : (s + 1) * TILE, :] = got[:, s * SLAB : (s + 1) * SLAB].astype(f32)
    turned = got[:, 256:512].astype(f32)
    for b in range(0, NT, 2):
        for q in range(4):
            pair = [turned[PLACES[u] * 8 : PLACES[u] * 8 + 8] for u in (b * 4 + q, b * 4 + 4 + q)]
            result[b * 8 : b * 8 + 16, q * COLS : (q + 1) * COLS] = jnp.concatenate(pair, axis=0).astype(bf16)


def exchange(x, axis):
    return lax.all_to_all(x, axis, split_axis=0, concat_axis=0, tiled=True)


def shards(activations, tile_owner, gradient, block_owner, eigen_basis, eigen_values):
    micro, tokens, width = activations.shape
    blocks, rows, cols = gradient.shape
    dp_count = lax.axis_size(DP)
    act = activations.reshape(micro * tokens, width)
    me = lax.axis_index(DP)
    y, low = lax.axis_index("y"), lax.axis_index("xl")
    high, core = lax.axis_index("xh"), lax.axis_index("c")
    group = high * 2 + core
    place = jnp.stack([low, group, (1 - high) * 2 + core, y]).astype(jnp.int32)
    tile_rank = slot_rank(tile_owner).astype(jnp.int32)
    block_rank = slot_rank(block_owner).astype(jnp.int32)

    near, far = sent_products(act, place)
    zero, one, up, down, three = along_products(act, place, (near,))
    near = lax.ppermute(near, "xl", [(0, 1), (1, 0)])
    far = lax.ppermute(far, ("xl", "xh"), [(i, 3 - i) for i in range(4)])

    [out] = call(
        scatter_kernel, [array((TILE, 640), bf16)], [], 0,
        place, eigen_basis, eigen_values, gradient.reshape(blocks * rows, cols), after=(up,),
    )
    own = kept_products(act, place, (out,))
    got = exchange(out, DP)
    [out] = call(
        forward_kernel, [array((TILE, 256), bf16)], [], 0,
        block_owner, block_rank, got, scalars=2, after=(near, far),
    )
    mine = exchange(out, DP)
    quarter = mine[:, :SLAB]
    others = [lax.ppermute(quarter, ("xh", "c"), [(i, i ^ k) for i in range(4)]) for k in (1, 2, 3)]
    my_block = jnp.asarray(np.array(UNIT) // 4, jnp.int32)[me]
    [rotated] = call(
        rotate_kernel, [array((TILE, COLS), bf16)], [((TILE, TILE), bf16)], 4 * TILE * TILE * COLS,
        jnp.stack([group, block_rank[my_block]]).astype(jnp.int32), mine, *others, got,
    )

    along = around_y(lambda: zero, lambda: one, up, down, lambda: three)
    half = along.shape[0] // 2
    sent = lax.dynamic_slice_in_dim(along, (1 - low) * half, half, 0)
    kept = lax.dynamic_slice_in_dim(along, low * half, half, 0)
    come = lax.ppermute(sent.astype(bf16), "xl", [(0, 1), (1, 0)])

    opposite = (own[2] + far[:64].astype(f32)).astype(bf16)
    across = around_y(
        lambda: own[0] + near[:64].astype(f32),
        lambda: own[1] + near[64:].astype(f32),
        opposite[:32],
        opposite[32:],
        lambda: own[3] + far[64:].astype(f32),
    )
    across, come = lax.optimization_barrier((across, come))
    along = kept + come.astype(f32)
    sums = exchange(jnp.concatenate([across.astype(bf16), along.astype(bf16)], axis=1), "z")

    [out] = call(
        functools.partial(pack_kernel, micro * tokens * dp_count),
        [array((TILE, 512), bf16)], [((8, UT * SLAB), f32), ((TILE, 256), f32)], 0,
        tile_owner, tile_rank, sums, rotated, scalars=2,
    )
    final = exchange(out, DP)
    factor, result = call(
        unpack_kernel, [array((SLOTS * TILE, SLAB), f32), array((blocks * rows, cols), bf16)], [], 0,
        final, scalars=0,
    )
    return factor.reshape(SLOTS, TILE, SLAB), result.reshape(blocks, rows, cols)


def solution(mesh):
    fine = Mesh(mesh.devices.reshape(4, 2, 8, 2, 2), ("y", "xl", "z", "xh", "c"))
    group = ("xh", "c")
    placed = (
        P(None, DP, None),
        P(),
        P(None, DP, group),
        P(),
        P(DP, None, None),
        P(DP, None),
    )
    return jax.shard_map(
        shards,
        mesh=fine,
        in_specs=placed,
        out_specs=(P(DP, None, group), P(None, DP, group)),
        check_vma=False,
    )
```
